32 devices in a mesh: sec: 4 (over y, core), mom: 2 (over x), en: 4 (over z).
Axes of the slice: x: 2, y: 2, z: 4, core: 2. Of those that a mesh axis runs over, the one named last changes fastest.
Arguments:
- green_blocks: bfloat16 [2, 32, 2, 128, 128], P('mom', ('sec', 'en')), may hold values from -6 to 6
- derivative: bfloat16 [3, 128, 128], replicated, may hold values from -0.5 to 0.5
- bare_phonon: float32 [4, 2, 2, 3, 3, 128], P('sec', 'mom'), may hold values from -4 to 4
- prior_polar: float32 [4, 2, 2, 3, 3, 128], P('sec', 'mom'), may hold values from -4 to 4
- offsets: int32 [4], replicated, may hold values from 1 to 2, as said below
- momenta: int32 [2, 2], replicated, may hold values from 0 to 1, as said below
Outputs:
- sigma: float32 [2, 32, 2, 128, 128], P('mom', ('sec', 'en'))
- polarization: float32 [4, 2, 3, 128], P('sec', 'mom')
The draws below stay inside these ranges and needn't reach their ends.
Inputs may be any that keep to these rules, and one draw needn't show every extreme that they name: `offsets`: every mode's offset lies in 1 to 2; some mode's offset equals 2 and another mode's equals 1. momenta[k, k'] = p((k - k') mod 2) for a permutation p of the 2 phonon momenta.
All inputs are finite; a program needn't handle non-finite values.
Results may differ from the reference program's by a relative error of at most 0.014.
Values may be sent and summed in bfloat16 or wider, within the bound.
A program may use at most 64 MiB of HBM per device.

```python
import math
import jax
import jax.numpy as jnp
from jax import lax

NB = 128
E_DEV = 2
NK = 2
NE = 32
NW = 4


def draw_offsets(key, part):
    base_key = jax.random.fold_in(key, 9173)
    first_key = jax.random.fold_in(base_key, 1)
    second_key = jax.random.fold_in(base_key, 2)
    third_key = jax.random.fold_in(base_key, 3)
    rotation = jax.random.randint(first_key, (), 0, E_DEV)
    extra = jax.random.randint(third_key, (NW,), 0, E_DEV)
    mode_ids = jnp.arange(NW)
    values = 1 + (mode_ids + rotation + extra) % E_DEV
    order = jax.random.permutation(second_key, NW)
    values = jnp.where(mode_ids == order[0], E_DEV, values)
    values = jnp.where(mode_ids == order[1], 1, values)
    return values.astype(jnp.int32)


def draw_momenta(key, part):
    labels = jax.random.permutation(jax.random.fold_in(key, 23), NK).astype(jnp.int32)
    row_ids = jnp.arange(NK, dtype=jnp.int32)[:, None]
    col_ids = jnp.arange(NK, dtype=jnp.int32)[None, :]
    return labels[(row_ids - col_ids) % NK].astype(jnp.int32)


def block_scale(stream_key, shape, pieces, smallest, largest):
    factor_of = 1.0
    for axis_at, shards_of in pieces:
        steps = jax.random.uniform(jax.random.fold_in(jax.random.fold_in(stream_key, 6), axis_at), (shards_of,), jnp.float32, smallest / len(pieces), largest / len(pieces))
        factor_of = factor_of * jnp.repeat(jnp.exp(steps), shape[axis_at] // shards_of).reshape((-1,) + (1,) * (len(shape) - 1 - axis_at))
    return factor_of


def gaussian(own_key, extent, deviation, most, pieces=(), held_as=jnp.bfloat16):
    drawn = deviation * jax.random.normal(own_key, extent, jnp.float32)
    if pieces:
        drawn = drawn * block_scale(own_key, extent, pieces, -0.22, 0.18)
    return jnp.clip(drawn, -most, most).astype(held_as)


def setup_inputs(seed: int = 0) -> dict:
    seeds = jax.random.split(jax.random.key(seed), 7)
    return {
        "green_blocks": gaussian(seeds[0], (NK, NE, 2, NB, NB), 1.0, 6.0, ((0, 2), (1, 16))),
        "derivative": gaussian(seeds[1], (3, NB, NB), NB ** -0.5, 0.5),
        "bare_phonon": gaussian(seeds[2], (NW, NK, 2, 3, 3, NB), 0.5, 4.0, ((0, 4), (1, 2)), jnp.float32),
        "prior_polar": gaussian(seeds[3], (NW, NK, 2, 3, 3, NB), 0.5, 4.0, ((0, 4), (1, 2)), jnp.float32),
        "offsets": draw_offsets(jax.random.fold_in(seeds[6], 71), 0),
        "momenta": draw_momenta(jax.random.fold_in(seeds[6], 71), 0),
    }


def contract(former, latter):
    return lax.optimization_barrier(jnp.sum(former[..., :, :, None, :] * latter[..., None, :, :, :], axis=-3))

def complex_product(former, latter):
    real_part = contract(former[..., 0, :, :, :], latter[..., 0, :, :, :]) - contract(former[..., 1, :, :, :], latter[..., 1, :, :, :])
    imag_part = contract(former[..., 0, :, :, :], latter[..., 1, :, :, :]) + contract(former[..., 1, :, :, :], latter[..., 0, :, :, :])
    return jnp.stack([real_part, imag_part], axis=-4)

def dyson_update(bare_phonon, prior_polar):
    return bare_phonon + complex_product(complex_product(bare_phonon, prior_polar), bare_phonon)

def flipped_products(blocks, derivative):
    flipped = jnp.einsum('ktcbx,ixa->kticab', blocks.astype(jnp.float32), derivative.astype(jnp.float32))
    sign_flip = jnp.array([1.0, -1.0], jnp.float32).reshape(1, 1, 1, 2, 1, 1)
    return (flipped * sign_flip).astype(jnp.bfloat16)

def mode_weights(chosen):
    real_part = chosen[:, :, 0]
    imag_part = chosen[:, :, 1]
    upper_part = jnp.stack([real_part, -imag_part], axis=2)
    lower_part = jnp.stack([imag_part, real_part], axis=2)
    return jnp.stack([upper_part, lower_part], axis=2)

def reference(green_blocks, derivative, bare_phonon, prior_polar, offsets, momenta):
    phonon = dyson_update(bare_phonon, prior_polar)
    phonon_table = jnp.transpose(phonon, (1, 0, 2, 3, 4, 5))
    flipped = flipped_products(green_blocks, derivative)
    momentum_ids = lax.broadcasted_iota(jnp.int32, (NK, NK), 1)

    def one_point(totals, source_index):
        sigma_sum, polar_sum = totals
        source = lax.dynamic_index_in_dim(green_blocks, source_index, 0, keepdims=False)
        column = lax.dynamic_index_in_dim(momenta, source_index, 1, keepdims=False)
        onehot = (column[:, None] == momentum_ids).astype(jnp.float32)
        chosen = jnp.einsum('kq,qmxija->kmxija', onehot, phonon_table, precision=lax.Precision.HIGHEST)
        blocks = jnp.einsum('iab,scbd->iscad', derivative.astype(jnp.float32), source.astype(jnp.float32)).astype(jnp.bfloat16)
        padded = jnp.pad(blocks, ((0, 0), (E_DEV, 0), (0, 0), (0, 0), (0, 0)))
        selected = jnp.stack([lax.dynamic_slice_in_dim(padded, E_DEV - offsets[mode_index], NE, 1) for mode_index in range(NW)], axis=2)
        weights = mode_weights(chosen)
        combined = jnp.einsum('kmxyija,itmyab->ktjxab', weights, selected.astype(jnp.float32), precision=lax.Precision.HIGHEST).astype(jnp.bfloat16)
        sigma_part = jnp.einsum('ktjxab,jbd->ktxad', combined.astype(jnp.float32), derivative.astype(jnp.float32))
        polar_part = jnp.einsum('itmcab,kticab->kmia', selected.astype(jnp.float32), flipped.astype(jnp.float32))
        polar_sum = polar_sum + jnp.einsum('kq,kmia->qmia', onehot, polar_part, precision=lax.Precision.HIGHEST)
        return ((sigma_sum + sigma_part, polar_sum), None)
    initial = (jnp.zeros((NK, NE, 2, NB, NB), jnp.float32), jnp.zeros((NK, NW, 3, NB), jnp.float32))
    (sigma_sum, polar_sum), _ = lax.scan(one_point, initial, jnp.arange(NK, dtype=jnp.int32))
    sigma_scale = 1.0 / math.sqrt(9.0 * NW * NK)
    polar_scale = 1.0 / math.sqrt(float(NK * NE * NB))
    polarization = jnp.transpose(polar_sum, (1, 0, 2, 3)) * polar_scale
    return (sigma_sum * sigma_scale, polarization)
```

```python
import functools
import math

import jax
import jax.numpy as jnp
from jax import lax
from jax.experimental import pallas as pl
from jax.experimental.pallas import tpu as pltpu
from jax.sharding import PartitionSpec as P

MESH = pl.DeviceIdType.MESH
STRIDE = 32


def kernel(
    sizes,
    scales,
    off_ref,
    mom_ref,
    g_ref,
    d_ref,
    bare_ref,
    prior_ref,
    sigma_ref,
    polar_ref,
    rim,
    near,
    phon,
    wbuf,
    mix,
    terms,
    psend,
    precv,
    bsend,
    brecv,
    rim_send,
    rim_recv,
    near_send,
    near_recv,
    phon_send,
    phon_recv,
    pol_send,
    pol_recv,
    sum_send,
    sum_recv,
):
    secs, points, ens, levels, modes, order = sizes
    sigma_scale, polar_scale = scales
    f32, bf16 = jnp.float32, jnp.bfloat16
    sec, mom, en = lax.axis_index("sec"), lax.axis_index("mom"), lax.axis_index("en")
    group = secs * points
    gid = sec * points + mom
    chain = sec * ens + en
    has_next = chain + 1 < secs * ens
    has_prev = chain > 0
    next_chain = lax.rem(chain + 1, secs * ens)
    prev_chain = lax.rem(chain + secs * ens - 1, secs * ens)

    def at_group(index):
        return {"sec": index // points, "mom": lax.rem(index, points), "en": en}

    def at_chain(index, m):
        return {"sec": index // ens, "mom": m, "en": lax.rem(index, ens)}

    def at_en(index):
        return {"sec": sec, "mom": mom, "en": index}

    barrier = pltpu.get_barrier_semaphore()
    for rel in range(1, group):
        pl.semaphore_signal(
            barrier, inc=1, device_id=at_group(lax.rem(gid + rel, group)), device_id_type=MESH
        )
    for rel in range(1, ens):
        pl.semaphore_signal(
            barrier, inc=1, device_id=at_en(lax.rem(en + rel, ens)), device_id_type=MESH
        )
    up = jnp.logical_and(has_next, en == ens - 1)
    down = jnp.logical_and(has_prev, en == 0)
    for r in range(points):
        m = lax.rem(mom + r, points)

        @pl.when(has_next if r else up)
        def _():
            pl.semaphore_signal(
                barrier, inc=1, device_id=at_chain(next_chain, m), device_id_type=MESH
            )

        @pl.when(has_prev if r else down)
        def _():
            pl.semaphore_signal(
                barrier, inc=1, device_id=at_chain(prev_chain, m), device_id_type=MESH
            )

    def product(former, latter):
        out = []
        for i in range(3):
            re = im = None
            for m in range(3):
                fr, fi = former[0][i][m : m + 1], former[1][i][m : m + 1]
                lr, li = latter[0][m], latter[1][m]
                tr, ti = fr * lr - fi * li, fr * li + fi * lr
                re = tr if re is None else re + tr
                im = ti if im is None else im + ti
            out.append((re, im))
        return [[o[0] for o in out], [o[1] for o in out]]

    bare = [[bare_ref[c, i] for i in range(3)] for c in range(2)]
    prior = [[prior_ref[c, i] for i in range(3)] for c in range(2)]
    full = product(product(bare, prior), bare)
    for c in range(2):
        for i in range(3):
            phon[gid, 9 * c + 3 * i : 9 * c + 3 * i + 3, :] = bare[c][i] + full[c][i]

    @pl.when(jnp.logical_not(has_prev))
    def _():
        rim[...] = jnp.zeros_like(rim)

    one = lambda flag: jnp.where(flag, 1, 0)
    pl.semaphore_wait(
        barrier,
        group
        + ens
        - 2
        + (points - 1) * (one(has_next) + one(has_prev))
        + one(up)
        + one(down),
    )

    def phon_copy(rel):
        return pltpu.make_async_remote_copy(
            src_ref=phon.at[gid],
            dst_ref=phon.at[gid],
            send_sem=phon_send.at[rel],
            recv_sem=phon_recv.at[rel],
            device_id=at_group(lax.rem(gid + rel, group)),
            device_id_type=MESH,
        )

    def rim_copy(r):
        return pltpu.make_async_remote_copy(
            src_ref=g_ref,
            dst_ref=rim.at[r],
            send_sem=rim_send.at[r],
            recv_sem=rim_recv.at[r],
            device_id=at_chain(next_chain, lax.rem(mom + points - r, points)),
            device_id_type=MESH,
        )

    def near_copy(r):
        return pltpu.make_async_remote_copy(
            src_ref=g_ref.at[pl.ds(0, levels - 1)],
            dst_ref=near.at[r],
            send_sem=near_send.at[r],
            recv_sem=near_recv.at[r],
            device_id=at_chain(chain, lax.rem(mom + points - r, points)),
            device_id_type=MESH,
        )

    for rel in range(1, group):
        phon_copy(rel).start()

    @pl.when(has_next)
    def _():
        for r in range(points - 1, -1, -1):
            rim_copy(r).start()

    for r in range(1, points):
        near_copy(r).start()

    d_f32 = [d_ref[i].astype(f32) for i in range(3)]
    d_side = jnp.concatenate([d_ref[i] for i in range(3)], axis=1)
    right = jnp.concatenate(
        [g_ref[e, c] if c == 0 else -g_ref[e, c] for e in range(levels) for c in range(2)], axis=0
    )

    for rel in range(1, group):
        phon_copy(rel).wait()

    is_off = [[(off_ref[w] == d + 1).astype(f32) for d in range(levels)] for w in range(modes)]
    is_mom = [
        [(mom_ref[mom, lax.rem(mom + r, points)] == q).astype(f32) for q in range(points)]
        for r in range(points)
    ]
    summed = [
        [
            sum(is_off[w][d] * phon[w * points + q] for w in range(modes))
            for q in range(points)
        ]
        for d in range(levels)
    ]
    for r in range(points):
        for d in range(levels):
            base = (r * levels + d) * STRIDE
            wbuf[base : base + 18, :] = sum(
                is_mom[r][q] * summed[d][q] for q in range(points)
            )
    per = order // STRIDE
    for r in range(points):
        for d in range(levels):
            slot = r * levels + d
            if slot % per == 0:
                turned = jnp.transpose(wbuf[slot * STRIDE : slot * STRIDE + order, :])
            base = (slot % per) * STRIDE
            left = (r * levels + d) * 2 * order
            for j in range(3):
                parts = []
                for c in range(2):
                    acc = None
                    for i in range(3):
                        col = base + 9 * c + 3 * i + j
                        term = turned[:, col : col + 1] * d_f32[i]
                        acc = term if acc is None else acc + term
                    parts.append(acc.astype(bf16))
                row = j * 2 * order
                mix[row : row + order, left : left + order] = parts[0]
                mix[row : row + order, left + order : left + 2 * order] = -parts[1]
                mix[row + order : row + 2 * order, left : left + order] = parts[1]
                mix[row + order : row + 2 * order, left + order : left + 2 * order] = parts[0]

    d_turned = [jnp.transpose(d_f32[i]) for i in range(3)]

    for r in range(1, points):
        near_copy(r).wait()

    @pl.when(has_next)
    def _():
        for r in range(points):
            rim_copy(r).wait_send()

    @pl.when(has_prev)
    def _():
        for r in range(points):
            rim_copy(r).wait_recv()

    def block(r, level, c):
        if level < 0:
            return rim[r, levels + level, c]
        return g_ref[level, c] if r == 0 else near[r, level, c]

    for r in range(points):
        for d in range(levels):
            slot = r * levels + d
            left = jnp.concatenate(
                [block(r, e - d - 1, c) for e in range(levels) for c in range(2)], axis=1
            )
            inner = jnp.dot(left, right, preferred_element_type=f32).astype(bf16)
            outer = jnp.dot(inner, d_side, preferred_element_type=f32)
            for i in range(3):
                terms[slot, i : i + 1, :] = jnp.sum(
                    outer[:, i * order : (i + 1) * order] * d_turned[i], axis=0, keepdims=True
                )
    for w in range(modes):
        by_point = [
            sum(is_off[w][d] * terms[r * levels + d] for d in range(levels))
            for r in range(points)
        ]
        for q in range(points):
            psend[w * points + q] = sum(is_mom[r][q] * by_point[r] for r in range(points))

    def pol_copy(rel):
        return pltpu.make_async_remote_copy(
            src_ref=psend.at[lax.rem(gid + rel, group)],
            dst_ref=precv.at[rel],
            send_sem=pol_send.at[rel],
            recv_sem=pol_recv.at[rel],
            device_id=at_group(lax.rem(gid + rel, group)),
            device_id_type=MESH,
        )

    def sum_copy(rel):
        return pltpu.make_async_remote_copy(
            src_ref=bsend,
            dst_ref=brecv.at[rel],
            send_sem=sum_send.at[rel],
            recv_sem=sum_recv.at[rel],
            device_id=at_en(lax.rem(en + rel, ens)),
            device_id_type=MESH,
        )

    for rel in range(1, group):
        pol_copy(rel).start()

    stacked = jnp.concatenate(
        [
            jnp.concatenate([block(r, e - d - 1, c) for e in range(levels)], axis=1)
            for r in range(points)
            for d in range(levels)
            for c in range(2)
        ],
        axis=0,
    )
    middle = jnp.dot(mix[...], stacked, preferred_element_type=f32).astype(bf16)

    for rel in range(1, group):
        pol_copy(rel).wait()
    share = psend[gid]
    for rel in range(1, group):
        share = share + precv[rel]
    bsend[...] = share
    for rel in range(1, ens):
        sum_copy(rel).start()

    d_down = jnp.concatenate([d_ref[j] for j in range(3)], axis=0)
    for e in range(levels):
        for x in range(2):
            lhs = jnp.concatenate(
                [
                    middle[
                        (2 * j + x) * order : (2 * j + x + 1) * order,
                        e * order : (e + 1) * order,
                    ]
                    for j in range(3)
                ],
                axis=1,
            )
            sigma_ref[e, x] = jnp.dot(lhs, d_down, preferred_element_type=f32) * sigma_scale

    for rel in range(1, ens):
        sum_copy(rel).wait()
    for rel in range(1, ens):
        share = share + brecv[rel]
    polar_ref[...] = share * polar_scale


def per_device(green_blocks, derivative, bare_phonon, prior_polar, offsets, momenta):
    secs, points, ens = (lax.axis_size(a) for a in ("sec", "mom", "en"))
    levels, order = green_blocks.shape[1], green_blocks.shape[-1]
    modes = offsets.shape[0]
    if green_blocks.shape[0] != 1 or bare_phonon.shape[:2] != (1, 1) or levels < 2:
        raise ValueError("unsupported placement")
    group = secs * points
    f32, bf16 = jnp.float32, jnp.bfloat16
    sizes = (secs, points, ens, levels, modes, order)
    scales = (
        1.0 / math.sqrt(9.0 * modes * points),
        1.0 / math.sqrt(float(points * levels * secs * ens * order)),
    )
    slots = points * levels
    wrows = -(-slots * STRIDE // order) * order
    vmem = pl.BlockSpec(memory_space=pltpu.VMEM)
    smem = pl.BlockSpec(memory_space=pltpu.SMEM)
    dma = pltpu.SemaphoreType.DMA
    sigma, polar = pl.pallas_call(
        functools.partial(kernel, sizes, scales),
        out_shape=(
            jax.ShapeDtypeStruct((levels, 2, order, order), f32),
            jax.ShapeDtypeStruct((3, order), f32),
        ),
        in_specs=[smem, smem, vmem, vmem, vmem, vmem],
        out_specs=(vmem, vmem),
        scratch_shapes=[
            pltpu.VMEM((points, levels, 2, order, order), bf16),
            pltpu.VMEM((points, levels - 1, 2, order, order), bf16),
            pltpu.VMEM((group, 18, order), f32),
            pltpu.VMEM((wrows, order), f32),
            pltpu.VMEM((6 * order, slots * 2 * order), bf16),
            pltpu.VMEM((slots, 3, order), f32),
            pltpu.VMEM((group, 3, order), f32),
            pltpu.VMEM((group, 3, order), f32),
            pltpu.VMEM((3, order), f32),
            pltpu.VMEM((ens, 3, order), f32),
            dma((points,)),
            dma((points,)),
            dma((points,)),
            dma((points,)),
            dma((group,)),
            dma((group,)),
            dma((group,)),
            dma((group,)),
            dma((ens,)),
            dma((ens,)),
        ],
        compiler_params=pltpu.CompilerParams(
            collective_id=0, has_side_effects=True, vmem_limit_bytes=40 * 1024 * 1024
        ),
        name="born_loop",
    )(
        offsets,
        momenta,
        green_blocks.reshape(green_blocks.shape[1:]),
        derivative,
        bare_phonon.reshape(bare_phonon.shape[2:]),
        prior_polar.reshape(prior_polar.shape[2:]),
    )
    return sigma[None], polar[None, None]


def solution(mesh):
    return jax.shard_map(
        per_device,
        mesh=mesh,
        in_specs=(
            P("mom", ("sec", "en"), None, None, None),
            P(),
            P("sec", "mom", None, None, None, None),
            P("sec", "mom", None, None, None, None),
            P(),
            P(),
        ),
        out_specs=(P("mom", ("sec", "en"), None, None, None), P("sec", "mom", None, None)),
        check_vma=False,
    )
```

```python
import functools
import math

import jax
import jax.numpy as jnp
from jax import lax
from jax.experimental import pallas as pl
from jax.experimental.pallas import tpu as pltpu
from jax.sharding import PartitionSpec as P

MESH = pl.DeviceIdType.MESH
STRIDE = 32


def kernel(
    sizes,
    scales,
    off_in,
    mom_in,
    g_in,
    d_in,
    bare_in,
    prior_in,
    sigma_ref,
    polar_ref,
    off_ref,
    mom_ref,
    g_ref,
    d_ref,
    bare_ref,
    prior_ref,
    rim,
    near,
    phon,
    wbuf,
    mix,
    terms,
    psend,
    precv,
    load_sem,
    rim_send,
    rim_recv,
    near_send,
    near_recv,
    phon_send,
    phon_recv,
    pol_send,
    pol_recv,
):
    secs, points, ens, levels, modes, order = sizes
    sigma_scale, polar_scale = scales
    f32, bf16 = jnp.float32, jnp.bfloat16
    sec, mom, en = lax.axis_index("sec"), lax.axis_index("mom"), lax.axis_index("en")
    group = secs * points
    gid = sec * points + mom
    chain = sec * ens + en
    has_next = chain + 1 < secs * ens
    has_prev = chain > 0
    next_chain = lax.rem(chain + 1, secs * ens)
    prev_chain = lax.rem(chain + secs * ens - 1, secs * ens)

    def at_group(index):
        return {"sec": index // points, "mom": lax.rem(index, points), "en": en}

    def at_chain(index, m):
        return {"sec": index // ens, "mom": m, "en": lax.rem(index, ens)}

    def at_en(index):
        return {"sec": sec, "mom": mom, "en": index}

    loads = [
        pltpu.make_async_copy(src, dst, load_sem.at[n])
        for n, (src, dst) in enumerate(
            [
                (bare_in, bare_ref),
                (prior_in, prior_ref),
                (off_in, off_ref),
                (mom_in, mom_ref),
                (g_in, g_ref),
                (d_in, d_ref),
            ]
        )
    ]
    for load in loads:
        load.start()

    total = group * ens
    me = gid * ens + en

    def everywhere(body):
        if total <= 64:
            for rel in range(1, total):
                body(rel)
        else:
            lax.fori_loop(1, total, lambda rel, _: (body(rel), 0)[1], 0)

    def at_rel(rel):
        index = lax.rem(me + rel, total)
        return {
            "sec": index // (points * ens),
            "mom": lax.rem(index // ens, points),
            "en": lax.rem(index, ens),
        }

    barrier = pltpu.get_barrier_semaphore()

    def greet(rel):
        pl.semaphore_signal(barrier, inc=1, device_id=at_rel(rel), device_id_type=MESH)

    everywhere(greet)

    for load in loads:
        load.wait()

    def product(former, latter):
        out = []
        for i in range(3):
            re = im = None
            for m in range(3):
                fr, fi = former[0][i][m : m + 1], former[1][i][m : m + 1]
                lr, li = latter[0][m], latter[1][m]
                tr, ti = fr * lr - fi * li, fr * li + fi * lr
                re = tr if re is None else re + tr
                im = ti if im is None else im + ti
            out.append((re, im))
        return [[o[0] for o in out], [o[1] for o in out]]

    bare = [[bare_ref[i, :, c, :] for i in range(3)] for c in range(2)]
    prior = [[prior_ref[i, :, c, :] for i in range(3)] for c in range(2)]
    full = product(product(bare, prior), bare)
    for c in range(2):
        for i in range(3):
            phon[gid, 9 * c + 3 * i : 9 * c + 3 * i + 3, :] = bare[c][i] + full[c][i]

    @pl.when(jnp.logical_not(has_prev))
    def _():
        rim[...] = jnp.zeros_like(rim)

    pl.semaphore_wait(barrier, total - 1)

    def phon_copy(rel):
        return pltpu.make_async_remote_copy(
            src_ref=phon.at[gid],
            dst_ref=phon.at[gid],
            send_sem=phon_send.at[rel],
            recv_sem=phon_recv.at[rel],
            device_id=at_group(lax.rem(gid + rel, group)),
            device_id_type=MESH,
        )

    def rim_copy(r):
        return pltpu.make_async_remote_copy(
            src_ref=g_ref,
            dst_ref=rim.at[r],
            send_sem=rim_send.at[r],
            recv_sem=rim_recv.at[r],
            device_id=at_chain(next_chain, lax.rem(mom + points - r, points)),
            device_id_type=MESH,
        )

    def near_copy(r):
        return pltpu.make_async_remote_copy(
            src_ref=g_ref.at[pl.ds(0, levels - 1)],
            dst_ref=near.at[r],
            send_sem=near_send.at[r],
            recv_sem=near_recv.at[r],
            device_id=at_chain(chain, lax.rem(mom + points - r, points)),
            device_id_type=MESH,
        )

    @pl.when(has_next)
    def _():
        for r in range(points - 1, -1, -1):
            rim_copy(r).start()

    for r in range(1, points):
        near_copy(r).start()

    for rel in range(1, group):
        phon_copy(rel).start()

    d_f32 = [d_ref[i].astype(f32) for i in range(3)]
    d_side = jnp.concatenate([d_ref[i] for i in range(3)], axis=1)
    right = jnp.concatenate(
        [g_ref[e, c] if c == 0 else -g_ref[e, c] for e in range(levels) for c in range(2)], axis=0
    )

    is_off = [[(off_ref[w] == d + 1).astype(f32) for d in range(levels)] for w in range(modes)]
    is_mom = [
        [(mom_ref[mom, lax.rem(mom + r, points)] == q).astype(f32) for q in range(points)]
        for r in range(points)
    ]
    d_turned = [jnp.transpose(d_f32[i]) for i in range(3)]

    for r in range(1, points):
        near_copy(r).wait()

    @pl.when(has_next)
    def _():
        for r in range(points):
            rim_copy(r).wait_send()

    @pl.when(has_prev)
    def _():
        for r in range(points):
            rim_copy(r).wait_recv()

    def block(r, level, c):
        if level < 0:
            return rim[r, levels + level, c]
        return g_ref[level, c] if r == 0 else near[r, level, c]

    for r in range(points):
        for d in range(levels):
            slot = r * levels + d
            left = jnp.concatenate(
                [block(r, e - d - 1, c) for e in range(levels) for c in range(2)], axis=1
            )
            inner = jnp.dot(left, right, preferred_element_type=f32).astype(bf16)
            outer = jnp.dot(inner, d_side, preferred_element_type=f32)
            for i in range(3):
                terms[slot, i : i + 1, :] = jnp.sum(
                    outer[:, i * order : (i + 1) * order] * d_turned[i], axis=0, keepdims=True
                )
    for w in range(modes):
        by_point = [
            sum(is_off[w][d] * terms[r * levels + d] for d in range(levels))
            for r in range(points)
        ]
        for q in range(points):
            psend[w * points + q] = sum(is_mom[r][q] * by_point[r] for r in range(points))

    def pol_copy(rel):
        return pltpu.make_async_remote_copy(
            src_ref=psend.at[lax.rem(me + rel, total) // ens],
            dst_ref=precv.at[rel],
            send_sem=pol_send.at[rel],
            recv_sem=pol_recv.at[rel],
            device_id=at_rel(rel),
            device_id_type=MESH,
        )

    everywhere(lambda rel: pol_copy(rel).start())

    for rel in range(1, group):
        phon_copy(rel).wait()

    summed = [
        [
            sum(is_off[w][d] * phon[w * points + q] for w in range(modes))
            for q in range(points)
        ]
        for d in range(levels)
    ]
    for r in range(points):
        for d in range(levels):
            base = (r * levels + d) * STRIDE
            wbuf[base : base + 18, :] = sum(
                is_mom[r][q] * summed[d][q] for q in range(points)
            )
    per = order // STRIDE
    for r in range(points):
        for d in range(levels):
            slot = r * levels + d
            if slot % per == 0:
                turned = jnp.transpose(wbuf[slot * STRIDE : slot * STRIDE + order, :])
            base = (slot % per) * STRIDE
            left = (r * levels + d) * 2 * order
            for j in range(3):
                parts = []
                for c in range(2):
                    acc = None
                    for i in range(3):
                        col = base + 9 * c + 3 * i + j
                        term = turned[:, col : col + 1] * d_f32[i]
                        acc = term if acc is None else acc + term
                    parts.append(acc.astype(bf16))
                row = j * 2 * order
                mix[row : row + order, left : left + order] = parts[0]
                mix[row : row + order, left + order : left + 2 * order] = -parts[1]
                mix[row + order : row + 2 * order, left : left + order] = parts[1]
                mix[row + order : row + 2 * order, left + order : left + 2 * order] = parts[0]

    stacked = jnp.concatenate(
        [
            jnp.concatenate([block(r, e - d - 1, c) for e in range(levels)], axis=1)
            for r in range(points)
            for d in range(levels)
            for c in range(2)
        ],
        axis=0,
    )
    middle = jnp.dot(mix[...], stacked, preferred_element_type=f32).astype(bf16)

    d_down = jnp.concatenate([d_ref[j] for j in range(3)], axis=0)
    for e in range(levels):
        for x in range(2):
            lhs = jnp.concatenate(
                [
                    middle[
                        (2 * j + x) * order : (2 * j + x + 1) * order,
                        e * order : (e + 1) * order,
                    ]
                    for j in range(3)
                ],
                axis=1,
            )
            sigma_ref[e, x] = jnp.dot(lhs, d_down, preferred_element_type=f32) * sigma_scale

    everywhere(lambda rel: pol_copy(rel).wait())
    precv[0] = psend[gid]
    share = jnp.sum(precv[...], axis=0)
    polar_ref[:, 0, :] = share * polar_scale


def per_device(green_blocks, derivative, bare_phonon, prior_polar, offsets, momenta):
    secs, points, ens = (lax.axis_size(a) for a in ("sec", "mom", "en"))
    levels, order = green_blocks.shape[1], green_blocks.shape[-1]
    modes = offsets.shape[0]
    if green_blocks.shape[0] != 1 or bare_phonon.shape[:2] != (1, 1) or levels < 2:
        raise ValueError("unsupported placement")
    group = secs * points
    f32, bf16 = jnp.float32, jnp.bfloat16
    sizes = (secs, points, ens, levels, modes, order)
    scales = (
        1.0 / math.sqrt(9.0 * modes * points),
        1.0 / math.sqrt(float(points * levels * secs * ens * order)),
    )
    slots = points * levels
    wrows = -(-slots * STRIDE // order) * order
    vmem = pl.BlockSpec(memory_space=pltpu.VMEM)
    hbm = pl.BlockSpec(memory_space=pltpu.HBM)
    dma = pltpu.SemaphoreType.DMA
    sigma, polar = pl.pallas_call(
        functools.partial(kernel, sizes, scales),
        out_shape=(
            jax.ShapeDtypeStruct((levels, 2, order, order), f32),
            jax.ShapeDtypeStruct((3, 1, order), f32),
        ),
        in_specs=[hbm] * 6,
        out_specs=(vmem, vmem),
        scratch_shapes=[
            pltpu.SMEM(offsets.shape, jnp.int32),
            pltpu.SMEM(momenta.shape, jnp.int32),
            pltpu.VMEM((levels, 2, order, order), bf16),
            pltpu.VMEM(derivative.shape, bf16),
            pltpu.VMEM((3, 3, 2, order), f32),
            pltpu.VMEM((3, 3, 2, order), f32),
            pltpu.VMEM((points, levels, 2, order, order), bf16),
            pltpu.VMEM((points, levels - 1, 2, order, order), bf16),
            pltpu.VMEM((group, 18, order), f32),
            pltpu.VMEM((wrows, order), f32),
            pltpu.VMEM((6 * order, slots * 2 * order), bf16),
            pltpu.VMEM((slots, 3, order), f32),
            pltpu.VMEM((group, 3, order), f32),
            pltpu.VMEM((group * ens, 3, order), f32),
            dma((6,)),
            dma((points,)),
            dma((points,)),
            dma((points,)),
            dma((points,)),
            dma((group,)),
            dma((group,)),
            dma((group * ens,)),
            dma((group * ens,)),
        ],
        compiler_params=pltpu.CompilerParams(
            collective_id=0, has_side_effects=True, vmem_limit_bytes=64 * 1024 * 1024 - 65536
        ),
        name="born_loop",
    )(
        offsets,
        momenta,
        green_blocks.reshape(green_blocks.shape[1:]),
        derivative,
        jnp.transpose(bare_phonon[0, 0], (1, 2, 0, 3)),
        jnp.transpose(prior_polar[0, 0], (1, 2, 0, 3)),
    )
    return sigma[None], polar.reshape(1, 1, 3, order)


def solution(mesh):
    return jax.shard_map(
        per_device,
        mesh=mesh,
        in_specs=(
            P("mom", ("sec", "en"), None, None, None),
            P(),
            P("sec", "mom", None, None, None, None),
            P("sec", "mom", None, None, None, None),
            P(),
            P(),
        ),
        out_specs=(P("mom", ("sec", "en"), None, None, None), P("sec", "mom", None, None)),
        check_vma=False,
    )
```

```python
import functools
import math

import jax
import jax.numpy as jnp
from jax import lax
from jax.experimental import pallas as pl
from jax.experimental.pallas import tpu as pltpu
from jax.sharding import PartitionSpec as P

MESH = pl.DeviceIdType.MESH
STRIDE = 32


def kernel(
    sizes,
    off_in,
    mom_in,
    g_in,
    d_in,
    bare_in,
    prior_in,
    sigma_ref,
    polar_ref,
    off_ref,
    mom_ref,
    g_ref,
    d_ref,
    bare_ref,
    prior_ref,
    rim,
    near,
    phon,
    wbuf,
    mix,
    terms,
    psend,
    precv,
    load_sem,
    rim_send,
    rim_recv,
    near_send,
    near_recv,
    phon_send,
    phon_recv,
    pol_send,
    pol_recv,
):
    secs, points, ens, levels, modes, order = sizes
    f32, bf16 = jnp.float32, jnp.bfloat16
    sec, mom, en = lax.axis_index("sec"), lax.axis_index("mom"), lax.axis_index("en")
    group = secs * points
    gid = sec * points + mom
    chain = sec * ens + en
    has_next = chain + 1 < secs * ens
    has_prev = chain > 0
    next_chain = lax.rem(chain + 1, secs * ens)
    prev_chain = lax.rem(chain + secs * ens - 1, secs * ens)

    def at_group(index):
        return {"sec": index // points, "mom": lax.rem(index, points), "en": en}

    def at_chain(index, m):
        return {"sec": index // ens, "mom": m, "en": lax.rem(index, ens)}

    def at_en(index):
        return {"sec": sec, "mom": mom, "en": index}

    loads = [
        pltpu.make_async_copy(src, dst, load_sem.at[n])
        for n, (src, dst) in enumerate(
            [
                (bare_in, bare_ref),
                (prior_in, prior_ref),
                (off_in, off_ref),
                (mom_in, mom_ref),
                (g_in, g_ref),
                (d_in, d_ref),
            ]
        )
    ]
    for load in loads:
        load.start()

    total = group * ens
    me = gid * ens + en

    def everywhere(body):
        if total <= 64:
            for rel in range(1, total):
                body(rel)
        else:
            lax.fori_loop(1, total, lambda rel, _: (body(rel), 0)[1], 0)

    def at_rel(rel):
        index = lax.rem(me + rel, total)
        return {
            "sec": index // (points * ens),
            "mom": lax.rem(index // ens, points),
            "en": lax.rem(index, ens),
        }

    barrier = pltpu.get_barrier_semaphore()

    def greet(rel):
        pl.semaphore_signal(barrier, inc=1, device_id=at_rel(rel), device_id_type=MESH)

    everywhere(greet)

    for load in loads:
        load.wait()

    def product(former, latter):
        out = []
        for i in range(3):
            re = im = None
            for m in range(3):
                fr, fi = former[0][i][m : m + 1], former[1][i][m : m + 1]
                lr, li = latter[0][m], latter[1][m]
                tr, ti = fr * lr - fi * li, fr * li + fi * lr
                re = tr if re is None else re + tr
                im = ti if im is None else im + ti
            out.append((re, im))
        return [[o[0] for o in out], [o[1] for o in out]]

    bare = [[bare_ref[i, :, c, :] for i in range(3)] for c in range(2)]
    prior = [[prior_ref[i, :, c, :] for i in range(3)] for c in range(2)]
    full = product(product(bare, prior), bare)
    for c in range(2):
        for i in range(3):
            phon[gid, 9 * c + 3 * i : 9 * c + 3 * i + 3, :] = bare[c][i] + full[c][i]

    @pl.when(jnp.logical_not(has_prev))
    def _():
        rim[...] = jnp.zeros_like(rim)

    pl.semaphore_wait(barrier, total - 1)

    def phon_copy(rel):
        return pltpu.make_async_remote_copy(
            src_ref=phon.at[gid],
            dst_ref=phon.at[gid],
            send_sem=phon_send.at[rel],
            recv_sem=phon_recv.at[rel],
            device_id=at_group(lax.rem(gid + rel, group)),
            device_id_type=MESH,
        )

    def rim_copy(r):
        return pltpu.make_async_remote_copy(
            src_ref=g_ref,
            dst_ref=rim.at[r],
            send_sem=rim_send.at[r],
            recv_sem=rim_recv.at[r],
            device_id=at_chain(next_chain, lax.rem(mom + points - r, points)),
            device_id_type=MESH,
        )

    def near_copy(r):
        return pltpu.make_async_remote_copy(
            src_ref=g_ref.at[pl.ds(0, levels - 1)],
            dst_ref=near.at[r],
            send_sem=near_send.at[r],
            recv_sem=near_recv.at[r],
            device_id=at_chain(chain, lax.rem(mom + points - r, points)),
            device_id_type=MESH,
        )

    @pl.when(has_next)
    def _():
        for r in range(points - 1, -1, -1):
            rim_copy(r).start()

    for r in range(1, points):
        near_copy(r).start()

    for rel in range(1, group):
        phon_copy(rel).start()

    d_f32 = [d_ref[i].astype(f32) for i in range(3)]
    d_side = jnp.concatenate([d_ref[i] for i in range(3)], axis=1)
    right = jnp.concatenate(
        [g_ref[e, c] if c == 0 else -g_ref[e, c] for e in range(levels) for c in range(2)], axis=0
    )

    is_off = [[(off_ref[w] == d + 1).astype(f32) for d in range(levels)] for w in range(modes)]
    is_mom = [
        [(mom_ref[mom, lax.rem(mom + r, points)] == q).astype(f32) for q in range(points)]
        for r in range(points)
    ]
    d_turned = [jnp.transpose(d_f32[i]) for i in range(3)]

    for r in range(1, points):
        near_copy(r).wait()

    @pl.when(has_next)
    def _():
        for r in range(points):
            rim_copy(r).wait_send()

    @pl.when(has_prev)
    def _():
        for r in range(points):
            rim_copy(r).wait_recv()

    def block(r, level, c):
        if level < 0:
            return rim[r, levels + level, c]
        return g_ref[level, c] if r == 0 else near[r, level, c]

    for r in range(points):
        for d in range(levels):
            slot = r * levels + d
            left = jnp.concatenate(
                [block(r, e - d - 1, c) for e in range(levels) for c in range(2)], axis=1
            )
            inner = jnp.dot(left, right, preferred_element_type=f32).astype(bf16)
            outer = jnp.dot(inner, d_side, preferred_element_type=f32)
            for i in range(3):
                terms[slot, i : i + 1, :] = jnp.sum(
                    outer[:, i * order : (i + 1) * order] * d_turned[i], axis=0, keepdims=True
                )
    for w in range(modes):
        by_point = [
            sum(is_off[w][d] * terms[r * levels + d] for d in range(levels))
            for r in range(points)
        ]
        for q in range(points):
            psend[w * points + q] = sum(is_mom[r][q] * by_point[r] for r in range(points))

    def pol_copy(rel):
        return pltpu.make_async_remote_copy(
            src_ref=psend.at[lax.rem(me + rel, total) // ens],
            dst_ref=precv.at[rel],
            send_sem=pol_send,
            recv_sem=pol_recv,
            device_id=at_rel(rel),
            device_id_type=MESH,
        )

    everywhere(lambda rel: pol_copy(rel).start())

    for rel in range(1, group):
        phon_copy(rel).wait()

    summed = [
        [
            sum(is_off[w][d] * phon[w * points + q] for w in range(modes))
            for q in range(points)
        ]
        for d in range(levels)
    ]
    for r in range(points):
        for d in range(levels):
            base = (r * levels + d) * STRIDE
            wbuf[base : base + 18, :] = sum(
                is_mom[r][q] * summed[d][q] for q in range(points)
            )
    per = order // STRIDE
    for r in range(points):
        for d in range(levels):
            slot = r * levels + d
            if slot % per == 0:
                turned = jnp.transpose(wbuf[slot * STRIDE : slot * STRIDE + order, :])
            base = (slot % per) * STRIDE
            left = (r * levels + d) * 2 * order
            for j in range(3):
                parts = []
                for c in range(2):
                    acc = None
                    for i in range(3):
                        col = base + 9 * c + 3 * i + j
                        term = turned[:, col : col + 1] * d_f32[i]
                        acc = term if acc is None else acc + term
                    parts.append(acc.astype(bf16))
                row = j * 2 * order
                mix[row : row + order, left : left + order] = parts[0]
                mix[row : row + order, left + order : left + 2 * order] = -parts[1]
                mix[row + order : row + 2 * order, left : left + order] = parts[1]
                mix[row + order : row + 2 * order, left + order : left + 2 * order] = parts[0]

    stacked = jnp.concatenate(
        [
            jnp.concatenate([block(r, e - d - 1, c) for e in range(levels)], axis=1)
            for r in range(points)
            for d in range(levels)
            for c in range(2)
        ],
        axis=0,
    )
    middle = jnp.dot(mix[...], stacked, preferred_element_type=f32).astype(bf16)

    d_down = jnp.concatenate([d_ref[j] for j in range(3)], axis=0)
    for e in range(levels):
        for x in range(2):
            lhs = jnp.concatenate(
                [
                    middle[
                        (2 * j + x) * order : (2 * j + x + 1) * order,
                        e * order : (e + 1) * order,
                    ]
                    for j in range(3)
                ],
                axis=1,
            )
            sigma_ref[e, x] = jnp.dot(lhs, d_down, preferred_element_type=f32)

    rest = precv.at[pl.ds(1, total - 1)]
    for sem in (pol_send, pol_recv):
        pltpu.make_async_copy(rest, rest, sem).wait()
    precv[0] = psend[gid]
    share = jnp.sum(precv[...], axis=0)
    polar_ref[:, 0, :] = share


def per_device(green_blocks, derivative, bare_phonon, prior_polar, offsets, momenta):
    secs, points, ens = (lax.axis_size(a) for a in ("sec", "mom", "en"))
    levels, order = green_blocks.shape[1], green_blocks.shape[-1]
    modes = offsets.shape[0]
    if green_blocks.shape[0] != 1 or bare_phonon.shape[:2] != (1, 1) or levels < 2:
        raise ValueError("unsupported placement")
    group = secs * points
    f32, bf16 = jnp.float32, jnp.bfloat16
    sizes = (secs, points, ens, levels, modes, order)
    scales = (
        1.0 / math.sqrt(9.0 * modes * points),
        1.0 / math.sqrt(float(points * levels * secs * ens * order)),
    )
    slots = points * levels
    wrows = -(-slots * STRIDE // order) * order
    vmem = pl.BlockSpec(memory_space=pltpu.VMEM)
    hbm = pl.BlockSpec(memory_space=pltpu.HBM)
    dma = pltpu.SemaphoreType.DMA
    sigma, polar = pl.pallas_call(
        functools.partial(kernel, sizes),
        out_shape=(
            jax.ShapeDtypeStruct((levels, 2, order, order), f32),
            jax.ShapeDtypeStruct((3, 1, order), f32),
        ),
        in_specs=[hbm] * 6,
        out_specs=(vmem, vmem),
        scratch_shapes=[
            pltpu.SMEM(offsets.shape, jnp.int32),
            pltpu.SMEM(momenta.shape, jnp.int32),
            pltpu.VMEM((levels, 2, order, order), bf16),
            pltpu.VMEM(derivative.shape, bf16),
            pltpu.VMEM((3, 3, 2, order), f32),
            pltpu.VMEM((3, 3, 2, order), f32),
            pltpu.VMEM((points, levels, 2, order, order), bf16),
            pltpu.VMEM((points, levels - 1, 2, order, order), bf16),
            pltpu.VMEM((group, 18, order), f32),
            pltpu.VMEM((wrows, order), f32),
            pltpu.VMEM((6 * order, slots * 2 * order), bf16),
            pltpu.VMEM((slots, 3, order), f32),
            pltpu.VMEM((group, 3, order), f32),
            pltpu.VMEM((group * ens, 3, order), f32),
            dma((6,)),
            dma((points,)),
            dma((points,)),
            dma((points,)),
            dma((points,)),
            dma((group,)),
            dma((group,)),
            dma,
            dma,
        ],
        compiler_params=pltpu.CompilerParams(
            collective_id=0, has_side_effects=True, vmem_limit_bytes=64 * 1024 * 1024 - 65536
        ),
        name="born_loop",
    )(
        offsets,
        momenta,
        green_blocks.reshape(green_blocks.shape[1:]),
        derivative,
        jnp.transpose(bare_phonon[0, 0], (1, 2, 0, 3)),
        jnp.transpose(prior_polar[0, 0], (1, 2, 0, 3)),
    )
    return sigma[None] * scales[0], polar.reshape(1, 1, 3, order) * scales[1]


def solution(mesh):
    return jax.shard_map(
        per_device,
        mesh=mesh,
        in_specs=(
            P("mom", ("sec", "en"), None, None, None),
            P(),
            P("sec", "mom", None, None, None, None),
            P("sec", "mom", None, None, None, None),
            P(),
            P(),
        ),
        out_specs=(P("mom", ("sec", "en"), None, None, None), P("sec", "mom", None, None)),
        check_vma=False,
    )
```

```python
import functools
import math

import jax
import jax.numpy as jnp
from jax import lax
from jax.experimental import pallas as pl
from jax.experimental.pallas import tpu as pltpu
from jax.sharding import PartitionSpec as P

MESH = pl.DeviceIdType.MESH
STRIDE = 32


def kernel(
    sizes,
    off_in,
    mom_in,
    g_in,
    d_in,
    bare_in,
    prior_in,
    sigma_ref,
    polar_ref,
    off_ref,
    mom_ref,
    g_ref,
    d_ref,
    bare_ref,
    prior_ref,
    rim,
    near,
    phon,
    wbuf,
    mix,
    terms,
    psend,
    precv,
    load_sem,
    rim_send,
    rim_recv,
    near_send,
    near_recv,
    phon_send,
    phon_recv,
    pol_send,
    pol_recv,
):
    secs, points, ens, levels, modes, order = sizes
    f32, bf16 = jnp.float32, jnp.bfloat16
    sec, mom, en = lax.axis_index("sec"), lax.axis_index("mom"), lax.axis_index("en")
    group = secs * points
    gid = sec * points + mom
    chain = sec * ens + en
    has_next = chain + 1 < secs * ens
    has_prev = chain > 0
    next_chain = lax.rem(chain + 1, secs * ens)
    prev_chain = lax.rem(chain + secs * ens - 1, secs * ens)

    def at_chain(index, m):
        return {"sec": index // ens, "mom": m, "en": lax.rem(index, ens)}

    loads = [
        pltpu.make_async_copy(src, dst, load_sem.at[n])
        for n, (src, dst) in enumerate(
            [
                (bare_in, bare_ref),
                (prior_in, prior_ref),
                (off_in, off_ref),
                (mom_in, mom_ref),
                (g_in, g_ref),
                (d_in, d_ref),
            ]
        )
    ]
    for load in loads:
        load.start()

    total = group * ens
    sec_at = [sec] + [lax.rem(sec + k, secs) for k in range(1, secs)]
    mom_at = [mom] + [lax.rem(mom + k, points) for k in range(1, points)]
    en_at = [en] + [lax.rem(en + k, ens) for k in range(1, ens)]
    row_at = [[a * points + b for b in mom_at] for a in sec_at]

    def everywhere(body):
        for rel in range(1, total):
            body(rel)

    def split(rel):
        return rel // (points * ens), rel // ens % points, rel % ens

    def at_rel(rel):
        a, b, c = split(rel)
        return {"sec": sec_at[a], "mom": mom_at[b], "en": en_at[c]}

    def row_of(rel):
        a, b, _ = split(rel)
        return row_at[a][b]

    barrier = pltpu.get_barrier_semaphore()

    def greet(rel):
        pl.semaphore_signal(barrier, inc=1, device_id=at_rel(rel), device_id_type=MESH)

    everywhere(greet)

    for load in loads:
        load.wait()

    def product(former, latter):
        out = []
        for i in range(3):
            re = im = None
            for m in range(3):
                fr, fi = former[0][i][m : m + 1], former[1][i][m : m + 1]
                lr, li = latter[0][m], latter[1][m]
                tr, ti = fr * lr - fi * li, fr * li + fi * lr
                re = tr if re is None else re + tr
                im = ti if im is None else im + ti
            out.append((re, im))
        return [[o[0] for o in out], [o[1] for o in out]]

    bare = [[bare_ref[i, :, c, :] for i in range(3)] for c in range(2)]
    prior = [[prior_ref[i, :, c, :] for i in range(3)] for c in range(2)]
    full = product(product(bare, prior), bare)
    for c in range(2):
        for i in range(3):
            phon[gid, 9 * c + 3 * i : 9 * c + 3 * i + 3, :] = bare[c][i] + full[c][i]

    @pl.when(jnp.logical_not(has_prev))
    def _():
        rim[...] = jnp.zeros_like(rim)

    pl.semaphore_wait(barrier, total - 1)

    def phon_copy(rel):
        return pltpu.make_async_remote_copy(
            src_ref=phon.at[gid],
            dst_ref=phon.at[gid],
            send_sem=phon_send.at[rel],
            recv_sem=phon_recv.at[rel],
            device_id=at_rel(rel * ens),
            device_id_type=MESH,
        )

    def rim_copy(r):
        return pltpu.make_async_remote_copy(
            src_ref=g_ref,
            dst_ref=rim.at[r],
            send_sem=rim_send.at[r],
            recv_sem=rim_recv.at[r],
            device_id=at_chain(next_chain, lax.rem(mom + points - r, points)),
            device_id_type=MESH,
        )

    def near_copy(r):
        return pltpu.make_async_remote_copy(
            src_ref=g_ref.at[pl.ds(0, levels - 1)],
            dst_ref=near.at[r],
            send_sem=near_send.at[r],
            recv_sem=near_recv.at[r],
            device_id=at_chain(chain, lax.rem(mom + points - r, points)),
            device_id_type=MESH,
        )

    @pl.when(has_next)
    def _():
        for r in range(points - 1, -1, -1):
            rim_copy(r).start()

    for r in range(1, points):
        near_copy(r).start()

    for rel in range(1, group):
        phon_copy(rel).start()

    d_f32 = [d_ref[i].astype(f32) for i in range(3)]
    d_side = jnp.concatenate([d_ref[i] for i in range(3)], axis=1)
    right = jnp.concatenate(
        [g_ref[e, c] if c == 0 else -g_ref[e, c] for e in range(levels) for c in range(2)], axis=0
    )

    is_off = [[(off_ref[w] == d + 1).astype(f32) for d in range(levels)] for w in range(modes)]
    is_mom = [
        [(mom_ref[mom, lax.rem(mom + r, points)] == q).astype(f32) for q in range(points)]
        for r in range(points)
    ]
    d_turned = [jnp.transpose(d_f32[i]) for i in range(3)]

    for r in range(1, points):
        near_copy(r).wait()

    @pl.when(has_next)
    def _():
        for r in range(points):
            rim_copy(r).wait_send()

    @pl.when(has_prev)
    def _():
        for r in range(points):
            rim_copy(r).wait_recv()

    def block(r, level, c):
        if level < 0:
            return rim[r, levels + level, c]
        return g_ref[level, c] if r == 0 else near[r, level, c]

    for r in range(points):
        for d in range(levels):
            slot = r * levels + d
            left = jnp.concatenate(
                [block(r, e - d - 1, c) for e in range(levels) for c in range(2)], axis=1
            )
            inner = jnp.dot(left, right, preferred_element_type=f32).astype(bf16)
            outer = jnp.dot(inner, d_side, preferred_element_type=f32)
            for i in range(3):
                terms[slot, i : i + 1, :] = jnp.sum(
                    outer[:, i * order : (i + 1) * order] * d_turned[i], axis=0, keepdims=True
                )
    for w in range(modes):
        by_point = [
            sum(is_off[w][d] * terms[r * levels + d] for d in range(levels))
            for r in range(points)
        ]
        for q in range(points):
            psend[w * points + q] = sum(is_mom[r][q] * by_point[r] for r in range(points))

    def pol_copy(rel):
        return pltpu.make_async_remote_copy(
            src_ref=psend.at[row_of(rel)],
            dst_ref=precv.at[rel],
            send_sem=pol_send,
            recv_sem=pol_recv,
            device_id=at_rel(rel),
            device_id_type=MESH,
        )

    everywhere(lambda rel: pol_copy(rel).start())

    for rel in range(1, group):
        phon_copy(rel).wait()

    summed = [
        [
            sum(is_off[w][d] * phon[w * points + q] for w in range(modes))
            for q in range(points)
        ]
        for d in range(levels)
    ]
    for r in range(points):
        for d in range(levels):
            base = (r * levels + d) * STRIDE
            wbuf[base : base + 18, :] = sum(
                is_mom[r][q] * summed[d][q] for q in range(points)
            )
    per = order // STRIDE
    for r in range(points):
        for d in range(levels):
            slot = r * levels + d
            if slot % per == 0:
                turned = jnp.transpose(wbuf[slot * STRIDE : slot * STRIDE + order, :])
            base = (slot % per) * STRIDE
            left = (r * levels + d) * 2 * order
            for j in range(3):
                parts = []
                for c in range(2):
                    acc = None
                    for i in range(3):
                        col = base + 9 * c + 3 * i + j
                        term = turned[:, col : col + 1] * d_f32[i]
                        acc = term if acc is None else acc + term
                    parts.append(acc.astype(bf16))
                row = j * 2 * order
                mix[row : row + order, left : left + order] = parts[0]
                mix[row : row + order, left + order : left + 2 * order] = -parts[1]
                mix[row + order : row + 2 * order, left : left + order] = parts[1]
                mix[row + order : row + 2 * order, left + order : left + 2 * order] = parts[0]

    stacked = jnp.concatenate(
        [
            jnp.concatenate([block(r, e - d - 1, c) for e in range(levels)], axis=1)
            for r in range(points)
            for d in range(levels)
            for c in range(2)
        ],
        axis=0,
    )
    middle = jnp.dot(mix[...], stacked, preferred_element_type=f32).astype(bf16)

    d_down = jnp.concatenate([d_ref[j] for j in range(3)], axis=0)
    for e in range(levels):
        for x in range(2):
            lhs = jnp.concatenate(
                [
                    middle[
                        (2 * j + x) * order : (2 * j + x + 1) * order,
                        e * order : (e + 1) * order,
                    ]
                    for j in range(3)
                ],
                axis=1,
            )
            sigma_ref[e, x] = jnp.dot(lhs, d_down, preferred_element_type=f32)

    rest = precv.at[pl.ds(1, total - 1)]
    for sem in (pol_send, pol_recv):
        pltpu.make_async_copy(rest, rest, sem).wait()
    precv[0] = psend[gid]
    share = jnp.sum(precv[...], axis=0)
    polar_ref[:, 0, :] = share


def per_device(green_blocks, derivative, bare_phonon, prior_polar, offsets, momenta):
    secs, points, ens = (lax.axis_size(a) for a in ("sec", "mom", "en"))
    levels, order = green_blocks.shape[1], green_blocks.shape[-1]
    modes = offsets.shape[0]
    if green_blocks.shape[0] != 1 or bare_phonon.shape[:2] != (1, 1) or levels < 2:
        raise ValueError("unsupported placement")
    group = secs * points
    f32, bf16 = jnp.float32, jnp.bfloat16
    sizes = (secs, points, ens, levels, modes, order)
    scales = (
        1.0 / math.sqrt(9.0 * modes * points),
        1.0 / math.sqrt(float(points * levels * secs * ens * order)),
    )
    slots = points * levels
    wrows = -(-slots * STRIDE // order) * order
    vmem = pl.BlockSpec(memory_space=pltpu.VMEM)
    hbm = pl.BlockSpec(memory_space=pltpu.HBM)
    dma = pltpu.SemaphoreType.DMA
    sigma, polar = pl.pallas_call(
        functools.partial(kernel, sizes),
        out_shape=(
            jax.ShapeDtypeStruct((levels, 2, order, order), f32),
            jax.ShapeDtypeStruct((3, 1, order), f32),
        ),
        in_specs=[hbm] * 6,
        out_specs=(vmem, vmem),
        scratch_shapes=[
            pltpu.SMEM(offsets.shape, jnp.int32),
            pltpu.SMEM(momenta.shape, jnp.int32),
            pltpu.VMEM((levels, 2, order, order), bf16),
            pltpu.VMEM(derivative.shape, bf16),
            pltpu.VMEM((3, 3, 2, order), f32),
            pltpu.VMEM((3, 3, 2, order), f32),
            pltpu.VMEM((points, levels, 2, order, order), bf16),
            pltpu.VMEM((points, levels - 1, 2, order, order), bf16),
            pltpu.VMEM((group, 18, order), f32),
            pltpu.VMEM((wrows, order), f32),
            pltpu.VMEM((6 * order, slots * 2 * order), bf16),
            pltpu.VMEM((slots, 3, order), f32),
            pltpu.VMEM((group, 3, order), f32),
            pltpu.VMEM((group * ens, 3, order), f32),
            dma((6,)),
            dma((points,)),
            dma((points,)),
            dma((points,)),
            dma((points,)),
            dma((group,)),
            dma((group,)),
            dma,
            dma,
        ],
        compiler_params=pltpu.CompilerParams(
            collective_id=0, has_side_effects=True, vmem_limit_bytes=64 * 1024 * 1024 - 65536
        ),
        name="born_loop",
    )(
        offsets,
        momenta,
        green_blocks.reshape(green_blocks.shape[1:]),
        derivative,
        jnp.transpose(bare_phonon[0, 0], (1, 2, 0, 3)),
        jnp.transpose(prior_polar[0, 0], (1, 2, 0, 3)),
    )
    return sigma[None] * scales[0], polar.reshape(1, 1, 3, order) * scales[1]


def solution(mesh):
    return jax.shard_map(
        per_device,
        mesh=mesh,
        in_specs=(
            P("mom", ("sec", "en"), None, None, None),
            P(),
            P("sec", "mom", None, None, None, None),
            P("sec", "mom", None, None, None, None),
            P(),
            P(),
        ),
        out_specs=(P("mom", ("sec", "en"), None, None, None), P("sec", "mom", None, None)),
        check_vma=False,
    )
```
